32 devices in a mesh: groups: 2 (over y), pool: 4 (over x, core), tp: 4 (over z).
Axes of the slice: x: 2, y: 2, z: 4, core: 2. Of those that a mesh axis runs over, the one named last changes fastest.
Arguments:
- queries: bfloat16 [8, 128, 16, 128], P(('groups', 'pool'), None, 'tp'), parts along dimension 0, may hold values from -8 to 8
- suffix_kv: bfloat16 [8, 128, 2, 256], P(('groups', 'pool')), parts along dimension 0, may hold values from -8 to 8
- kv_pool: bfloat16 [192, 2, 128, 256], P(('groups', 'pool', 'tp')), parts along dimension 0, may hold values from -6 to 6
- page_map: int32 [192], P('groups'), parts along dimension 0, may hold values from 0 to 95, as said below
- hit_pages: int32 [8, 16], P('groups'), parts along dimension 0, may hold values from 0 to 95, as said below
- suffix_lengths: int32 [8], P(('groups', 'pool')), parts along dimension 0, may hold values from 32 to 128, as said below
- out_weight: bfloat16 [2048, 8192], P('tp'), may hold values from -0.5 to 0.5
Outputs:
- layer_update: bfloat16 [8, 128, 8192], P(('groups', 'pool'), 'tp'), parts along dimension 0
The draws below stay inside these ranges and needn't reach their ends.
There are 2 independent parts, one for each index of `groups`. The reference program is written for one: setup_inputs(seed, part) draws one part's arguments, and reference() takes and returns one part's arrays. A program takes and returns all parts, laid end to end along the dimension named above; an argument that names none is the same for every part. Nothing has to cross between parts.
Inputs may be any that keep to these rules, and one draw needn't show every extreme that they name: `page_map`: a permutation of the physical pages. `hit_pages`: the 16 logical pages of one session are different; through page_map at most 2 pages of one session lie on one device, and one device holds exactly 2 pages of every session. `suffix_lengths`: some session has all 128 suffix tokens live.
All inputs are finite; a program needn't handle non-finite values.
Results may differ from the reference program's by a relative error of at most 0.012.
Values may be sent and summed in bfloat16 or wider, within the bound.
A program may use at most 128 MiB of HBM per device.

```python
import math
import jax
import jax.numpy as jnp
from jax import lax

D = 8192
HD = 128
PAGE = 128
CAP = 2
PDEV = 6
SUF = 128
QH = 16
KVH = 2
SESSIONS = 4
POOL_PAGES = 96
PREFIX_PAGES = 16


def page_layout(key):
    owners = POOL_PAGES // PDEV
    perm_key, hot_key, start_key, prio_key, order_key = jax.random.split(key, 5)
    page_map = jax.random.permutation(perm_key, POOL_PAGES).astype(jnp.int32)
    hot_owner = jax.random.randint(hot_key, (), 0, owners)
    starts = jax.random.randint(start_key, (SESSIONS, owners), 0, PDEV)
    owner_ids = jnp.arange(owners, dtype=jnp.int32)
    starts = jnp.where(owner_ids[None, :] == hot_owner, starts[0:1, :], starts)
    offsets = jnp.arange(CAP, dtype=jnp.int32)
    physical = owner_ids[None, :, None] * PDEV + (starts[:, :, None] + offsets[None, None, :]) % PDEV
    prio_keys = jax.random.split(prio_key, SESSIONS)
    priority = jax.vmap(lambda one_key: jax.random.permutation(one_key, owners * CAP))(prio_keys) + 1
    priority = priority.reshape(SESSIONS, owners, CAP)
    priority = jnp.where(owner_ids[None, :, None] == hot_owner, 0, priority)
    picked = jnp.argsort(priority.reshape(SESSIONS, owners * CAP), axis=1, stable=True)[:, :PREFIX_PAGES]
    chosen = jnp.take_along_axis(physical.reshape(SESSIONS, owners * CAP), picked, axis=1)
    shuffle_keys = jax.random.split(order_key, SESSIONS)
    shuffle = jax.vmap(lambda one_key: jax.random.permutation(one_key, PREFIX_PAGES))(shuffle_keys)
    chosen = jnp.take_along_axis(chosen, shuffle, axis=1)
    logical = jnp.argsort(page_map, stable=True).astype(jnp.int32)
    return (page_map, jnp.take(logical, chosen, axis=0).astype(jnp.int32))


def draw_page_map(key, part):
    page_map, hits = page_layout(key)
    return page_map


def draw_hit_pages(key, part):
    page_map, hits = page_layout(key)
    return hits


def draw_suffix_lengths(key, part):
    key = jax.random.fold_in(key, 5)
    first_key, second_key = jax.random.split(key)
    lengths = jax.random.randint(first_key, (SESSIONS,), SUF // 4, SUF + 1)
    longest = jax.random.randint(second_key, (), 0, SESSIONS)
    return jnp.where(jnp.arange(SESSIONS) == longest, SUF, lengths).astype(jnp.int32)


def draw_queries(key, part):
    key = jax.random.fold_in(key, 1)
    shape = (SESSIONS, SUF, QH, HD)
    values = 1.5 * jax.random.truncated_normal(key, -4.0, 4.0, shape)
    return values.astype(jnp.bfloat16)


def draw_kv_pool(key, part):
    key = jax.random.fold_in(key, 2)
    shape = (POOL_PAGES, KVH, PAGE, 2 * HD)
    values = jax.random.truncated_normal(key, -4.0, 4.0, shape)
    return values.astype(jnp.bfloat16)


def block_levels(key, shape, shards, low, high):
    factor_of, own = 1.0, jax.random.fold_in(key, 6)
    for dim, parts in shards:
        steps = jnp.exp(jax.random.uniform(jax.random.fold_in(own, dim), (parts,), jnp.float32, low / len(shards), high / len(shards)))
        factor_of = factor_of * jnp.repeat(steps, shape[dim] // parts).reshape([-1 if axis == dim else 1 for axis in range(len(shape))])
    return factor_of


def normal_values(own_key, dims, spread, most, cuts=(), kind=jnp.bfloat16):
    loudness = block_levels(own_key, dims, cuts, -0.22, 0.18) if cuts else 1.0
    drawn = jax.random.normal(own_key, dims, jnp.float32) * spread * loudness
    return jnp.minimum(jnp.maximum(drawn, -most), most).astype(kind)


def setup_inputs(seed: int = 0, part: int = 0) -> dict:
    key_list = jax.random.split(jax.random.key(seed), 8)
    part_keys = jax.random.split(jax.random.fold_in(key_list[7], part), 8)
    queries = draw_queries(jax.random.fold_in(jax.random.fold_in(key_list[7], part), 71), part)
    suffix_kv = normal_values(part_keys[1], (SESSIONS, SUF, KVH, 2 * HD), 2.0, 8.0, ((0, 4),))
    kv_pool = draw_kv_pool(jax.random.fold_in(jax.random.fold_in(key_list[7], part), 71), part)
    page_map = draw_page_map(jax.random.fold_in(jax.random.fold_in(key_list[7], part), 71), part)
    hit_pages = draw_hit_pages(jax.random.fold_in(jax.random.fold_in(key_list[7], part), 71), part)
    suffix_lengths = draw_suffix_lengths(jax.random.fold_in(jax.random.fold_in(key_list[7], part), 71), part)
    out_weight = normal_values(key_list[6], (QH * HD, D), HD ** -0.5, 0.5, ((0, 4),))
    return dict(queries=queries, suffix_kv=suffix_kv, kv_pool=kv_pool, page_map=page_map, hit_pages=hit_pages, suffix_lengths=suffix_lengths, out_weight=out_weight)


NEG_FILL = -1e+30

def one_session(queries_one, suffix_one, physical_one, length_one, kv_pool, out_weight):
    prefix = jnp.take(kv_pool, physical_one, axis=0)
    prefix = jnp.transpose(prefix, (1, 0, 2, 3)).reshape(KVH, PREFIX_PAGES * PAGE, 2 * HD)
    suffix_heads = jnp.transpose(suffix_one, (1, 0, 2))
    group_size = QH // KVH
    grouped = jnp.transpose(queries_one.reshape(SUF, KVH, group_size, HD), (1, 2, 0, 3))
    positions = jnp.arange(SUF, dtype=jnp.int32)
    causal = positions[None, :] <= positions[:, None]
    visible = jnp.concatenate([jnp.ones((SUF, PREFIX_PAGES * PAGE), dtype=bool), causal], axis=1)

    def per_head(operands):
        query_group, prefix_head, suffix_head = operands
        keys_all = jnp.concatenate([prefix_head, suffix_head], axis=0)
        scores = jnp.einsum('gqd,kd->gqk', query_group.astype(jnp.float32), keys_all[:, :HD].astype(jnp.float32))
        scores = scores / math.sqrt(HD)
        scores = jnp.where(visible[None], scores, NEG_FILL)
        peak_score = lax.optimization_barrier(jnp.max(scores, axis=2))
        weights = jnp.where(visible[None], jnp.exp(scores - peak_score[..., None]), 0.0)
        total_weight = lax.optimization_barrier(jnp.sum(weights, axis=2))
        rounded = lax.optimization_barrier(weights.astype(jnp.bfloat16))
        attended = jnp.einsum('gqk,kd->gqd', rounded.astype(jnp.float32), keys_all[:, HD:].astype(jnp.float32))
        return (attended / total_weight[..., None]).astype(jnp.bfloat16)
    attended = lax.map(per_head, (grouped, prefix, suffix_heads))
    flat_rows = jnp.transpose(attended, (2, 0, 1, 3)).reshape(SUF, QH * HD)
    mixed_rows = jnp.dot(flat_rows, out_weight, preferred_element_type=jnp.float32)
    live_rows = positions < length_one
    return jnp.where(live_rows[:, None], mixed_rows, 0.0).astype(jnp.bfloat16)

def reference(queries, suffix_kv, kv_pool, page_map, hit_pages, suffix_lengths, out_weight):
    physical = jnp.take(page_map, hit_pages, axis=0)

    def session_step(operands):
        queries_one, suffix_one, physical_one, length_one = operands
        return one_session(queries_one, suffix_one, physical_one, length_one, kv_pool, out_weight)
    return lax.map(session_step, (queries, suffix_kv, physical, suffix_lengths))
```

```python
import functools
import math

import jax
import jax.numpy as jnp
from jax import lax
from jax.experimental import pallas as pl
from jax.experimental.pallas import tpu as pltpu
from jax.sharding import PartitionSpec as P

CAP = 2
STAT = 8
LANES = 128
NEG_FILL = -1e30
MESH = pl.DeviceIdType.MESH
F32 = jnp.float32
BF16 = jnp.bfloat16


def kernel(
    pools, tps, block,
    map_ref, hit_ref, len_ref, q_ref, suf_ref, pool_ref, w_hbm,
    out_ref,
    w_ref, kv, kv_send, q_all, o_send, o_recv, s_send, s_recv, o_suf, attn, part, own, c_send, c_up, c_dn,
    w_sem, kv_ss, kv_rs, q_ss, q_rs, o_ss, o_rs, s_ss, s_rs, c_ss, up_rs, dn_rs,
):
    me_p, me = lax.axis_index("pool"), lax.axis_index("tp")
    pages_dev, kv_heads, page, width = pool_ref.shape
    hd = width // 2
    heads, rows, _ = q_ref.shape
    hits = hit_ref.shape[1]
    group = heads * tps // kv_heads
    blocks = own.shape[0]
    rows_dev = rows // tps
    scale = math.log2(math.e) / math.sqrt(hd)

    w_copy = pltpu.make_async_copy(w_hbm, w_ref, w_sem)
    w_copy.start()

    barrier = pltpu.get_barrier_semaphore()
    for d in range(1, pools):
        pl.semaphore_signal(barrier, inc=1, device_id={"pool": lax.rem(me_p + d, pools)}, device_id_type=MESH)
    for d in range(1, tps):
        pl.semaphore_signal(barrier, inc=1, device_id={"tp": lax.rem(me + d, tps)}, device_id_type=MESH)
    pl.semaphore_wait(barrier, pools + tps - 2)

    def q_copy(d):
        return pltpu.make_async_remote_copy(
            src_ref=q_ref, dst_ref=q_all.at[d - 1], send_sem=q_ss.at[d - 1], recv_sem=q_rs.at[d - 1],
            device_id={"tp": lax.rem(me + d, tps)}, device_id_type=MESH,
        )

    def kv_copy(d):
        return pltpu.make_async_remote_copy(
            src_ref=kv_send.at[d - 1], dst_ref=kv.at[d], send_sem=kv_ss.at[d - 1], recv_sem=kv_rs.at[d - 1],
            device_id={"pool": lax.rem(me_p + d, pools)}, device_id_type=MESH,
        )

    base = (me_p * tps + me) * pages_dev

    def choose(session):
        def body(i, carry):
            first, second, rank = carry
            local = map_ref[hit_ref[session, i]] - base
            owned = jnp.logical_and(local >= 0, local < pages_dev)
            first = jnp.where(jnp.logical_and(owned, rank == 0), local, first)
            second = jnp.where(jnp.logical_and(owned, rank == 1), local, second)
            return first, second, rank + owned.astype(jnp.int32)

        zero = jnp.int32(0)
        return lax.fori_loop(0, hits, body, (zero, zero, zero), unroll=hits <= 16)[:2]

    order = sorted(range(1, pools), key=lambda d: -min(d, pools - d))
    for d in order:
        first, second = choose(lax.rem(me_p + d, pools))
        kv_send[d - 1, 0] = pool_ref[first]
        kv_send[d - 1, 1] = pool_ref[second]
        kv_copy(d).start()
    for d in range(1, tps):
        q_copy(d).start()
    first, second = choose(me_p)
    kv[0, 0] = pool_ref[first]
    kv[0, 1] = pool_ref[second]

    bases = [(lax.rem(me_p + pools - d, pools) * tps + me) * pages_dev for d in range(pools)]

    def count(i, carry):
        physical = map_ref[hit_ref[me_p, i]]
        return tuple(
            c + jnp.logical_and(physical >= b, physical < b + pages_dev).astype(jnp.int32)
            for c, b in zip(carry, bases)
        )

    counts = lax.fori_loop(0, hits, count, tuple(jnp.int32(0) for _ in bases), unroll=hits <= 16)
    lane2 = lax.broadcasted_iota(jnp.int32, (1, CAP * page), 1)
    biases = [
        jnp.where(lane2 < page, jnp.where(c > 0, 0.0, NEG_FILL), jnp.where(c > 1, 0.0, NEG_FILL)).astype(F32)
        for c in counts
    ]

    def softmax(scores, values):
        top = functools.reduce(jnp.maximum, scores)
        peak = jnp.max(top, axis=1, keepdims=True) * scale
        weights = [jnp.exp2(s * scale - peak) for s in scores]
        total = jnp.sum(functools.reduce(jnp.add, weights), axis=1, keepdims=True)
        acc = functools.reduce(
            jnp.add,
            [jnp.dot(x.astype(BF16), v, preferred_element_type=F32) for x, v in zip(weights, values)],
        )
        return acc / total, peak + jnp.log2(total)

    def dot_t(a, b):
        return lax.dot_general(a, b, (((1,), (1,)), ((), ())), preferred_element_type=F32)

    q_own = q_ref[...].reshape(heads * rows, hd)
    scores = dot_t(q_own, suf_ref[:, :hd])
    row = lax.broadcasted_iota(jnp.int32, (heads, rows, rows), 1).reshape(heads * rows, rows)
    column = lax.broadcasted_iota(jnp.int32, (heads * rows, rows), 1)
    scores = jnp.where(column <= row, scores, NEG_FILL)
    att_suf, lse_suf = softmax([scores], [suf_ref[:, hd:]])
    o_suf[...] = att_suf

    def prefix(q, rank):
        g = lax.div(rank * heads, group)
        keys, values = [], []
        for d in range(pools):
            both = kv[d, :, g].reshape(CAP * page, width)
            keys.append(both[:, :hd])
            values.append(both[:, hd:])
        return softmax([dot_t(q, k) + b for k, b in zip(keys, biases)], values)

    for d in range(1, pools):
        kv_copy(d).wait_recv()
    for d in range(s_recv.shape[0]):
        if d >= tps - 1:
            s_recv[d] = jnp.zeros_like(s_recv[d])

    def o_copy(d):
        return pltpu.make_async_remote_copy(
            src_ref=o_send.at[d - 1], dst_ref=o_recv.at[d - 1], send_sem=o_ss.at[d - 1], recv_sem=o_rs.at[d - 1],
            device_id={"tp": lax.rem(me + d, tps)}, device_id_type=MESH,
        )

    def s_copy(d):
        return pltpu.make_async_remote_copy(
            src_ref=s_send.at[d - 1], dst_ref=s_recv.at[d - 1], send_sem=s_ss.at[d - 1], recv_sem=s_rs.at[d - 1],
            device_id={"tp": lax.rem(me + d, tps)}, device_id_type=MESH,
        )

    lane = lax.broadcasted_iota(jnp.int32, (rows, LANES), 1)

    @pl.loop(1, tps)
    def _(d):
        q_copy(tps - d).wait_recv()
        att, lse = prefix(q_all[tps - d - 1].reshape(heads * rows, hd), lax.rem(me + d, tps))
        o_send[d - 1] = att.astype(BF16).reshape(heads, rows, hd)
        o_copy(d).start()
        tile = jnp.zeros((rows, LANES), F32)
        for j in range(heads):
            tile = jnp.where(lane == j, lse[j * rows:(j + 1) * rows], tile)
        s_send[d - 1] = tile.T[:STAT]
        s_copy(d).start()

    att_own, lse_own = prefix(q_own, me)

    for d in range(1, tps):
        o_copy(d).wait_recv()
        s_copy(d).wait_recv()
    stats = s_recv[...].reshape(LANES, rows).T
    live = lax.broadcasted_iota(jnp.int32, (rows, 1), 0) < len_ref[0]
    for j in range(heads):
        here = slice(j * rows, (j + 1) * rows)
        logs = [lse_own[here], lse_suf[here]] + [
            stats[:, (d - 1) * STAT + j:(d - 1) * STAT + j + 1] for d in range(1, tps)
        ]
        parts = [att_own[here], o_suf[here]] + [o_recv[d - 1, j].astype(F32) for d in range(1, tps)]
        peak = functools.reduce(jnp.maximum, logs)
        shares = [jnp.exp2(x - peak) for x in logs]
        total = functools.reduce(jnp.add, shares)
        mixed = functools.reduce(jnp.add, [s * o for s, o in zip(shares, parts)]) / total
        attn[:, j * hd:(j + 1) * hd] = jnp.where(live, mixed, 0.0).astype(BF16)

    w_copy.wait()

    def c_copy(t, b, up):
        landing, sem, to = (c_up, up_rs, me + 1) if up else (c_dn, dn_rs, me + tps - 1)
        return pltpu.make_async_remote_copy(
            src_ref=c_send.at[t, b], dst_ref=landing.at[t, b], send_sem=c_ss.at[t, b], recv_sem=sem.at[t, b],
            device_id={"tp": lax.rem(to, tps)}, device_id_type=MESH,
        )

    def pass_on(t, b, up):
        first_one = me == 0 if up else me == tps - 1

        @pl.when(first_one)
        def _():
            c_send[t, b] = part[t].astype(BF16)

        @pl.when(jnp.logical_not(first_one))
        def _():
            c_copy(t, b, up).wait_recv()
            landing = c_up if up else c_dn
            c_send[t, b] = (part[t] + landing[t, b].astype(F32)).astype(BF16)

        c_copy(t, b, up).start()

    @pl.loop(0, blocks)
    def _(b):
        columns = pl.ds(pl.multiple_of(b * block, block), block)
        product = jnp.dot(attn[...], w_ref[:, columns], preferred_element_type=F32)
        for t in range(tps):
            part[t] = product[t * rows_dev:(t + 1) * rows_dev]
        own[b] = part[me]
        for far in range(tps - 1, 0, -1):
            @pl.when(me + far < tps)
            def _():
                pass_on(me + far, b, True)

            @pl.when(me >= far)
            def _():
                pass_on(me - far, b, False)

    @pl.loop(0, blocks)
    def _(b):
        @pl.when(me > 0)
        def _():
            c_copy(me, b, True).wait_recv()
            own[b] = own[b] + c_up[me, b].astype(F32)

        @pl.when(me < tps - 1)
        def _():
            c_copy(me, b, False).wait_recv()
            own[b] = own[b] + c_dn[me, b].astype(F32)

        out_ref[:, pl.ds(pl.multiple_of(b * block, block), block)] = own[b].astype(BF16)

    for d in range(1, pools):
        kv_copy(d).wait_send()
    for d in range(1, tps):
        q_copy(d).wait_send()
        o_copy(d).wait_send()
        s_copy(d).wait_send()

    @pl.loop(0, blocks)
    def _(b):
        for far in range(1, tps):
            @pl.when(me + far < tps)
            def _():
                c_copy(me + far, b, True).wait_send()

            @pl.when(me >= far)
            def _():
                c_copy(me - far, b, False).wait_send()


def per_device(pools, tps, queries, suffix_kv, kv_pool, page_map, hit_pages, suffix_lengths, out_weight):
    pages_dev, kv_heads, page, width = kv_pool.shape
    hd = width // 2
    rows, heads = queries.shape[1], queries.shape[2]
    model = out_weight.shape[1]
    block = min(1024, model)
    blocks = model // block
    rows_dev = rows // tps
    group = heads * tps // kv_heads
    q = jnp.transpose(queries[0], (1, 0, 2))
    suffix = lax.dynamic_index_in_dim(
        suffix_kv[0], lax.axis_index("tp") * heads // group, 1, keepdims=False
    )
    vmem = pl.BlockSpec(memory_space=pltpu.VMEM)
    smem = pl.BlockSpec(memory_space=pltpu.SMEM)
    dma = pltpu.SemaphoreType.DMA
    chain = (tps, blocks, rows_dev, block)
    out = pl.pallas_call(
        functools.partial(kernel, pools, tps, block),
        out_shape=jax.ShapeDtypeStruct((rows_dev, model), BF16),
        in_specs=[smem, smem, smem, vmem, vmem, vmem, pl.BlockSpec(memory_space=pl.ANY)],
        out_specs=vmem,
        scratch_shapes=[
            pltpu.VMEM(out_weight.shape, BF16),
            pltpu.VMEM((pools, CAP, kv_heads, page, width), BF16),
            pltpu.VMEM((pools - 1, CAP, kv_heads, page, width), BF16),
            pltpu.VMEM((tps - 1, heads, rows, hd), BF16),
            pltpu.VMEM((tps - 1, heads, rows, hd), BF16),
            pltpu.VMEM((tps - 1, heads, rows, hd), BF16),
            pltpu.VMEM((tps - 1, STAT, rows), F32),
            pltpu.VMEM((LANES // STAT, STAT, rows), F32),
            pltpu.VMEM((heads * rows, hd), F32),
            pltpu.VMEM((rows, heads * hd), BF16),
            pltpu.VMEM((tps, rows_dev, block), F32),
            pltpu.VMEM((blocks, rows_dev, block), F32),
            pltpu.VMEM(chain, BF16),
            pltpu.VMEM(chain, BF16),
            pltpu.VMEM(chain, BF16),
            dma,
            dma((pools - 1,)), dma((pools - 1,)),
            dma((tps - 1,)), dma((tps - 1,)),
            dma((tps - 1,)), dma((tps - 1,)),
            dma((tps - 1,)), dma((tps - 1,)),
            dma((tps, blocks)), dma((tps, blocks)), dma((tps, blocks)),
        ],
        compiler_params=pltpu.CompilerParams(
            collective_id=0, has_side_effects=True, vmem_limit_bytes=56 * 1024 * 1024
        ),
        cost_estimate=pl.CostEstimate(flops=3 * 10**9, bytes_accessed=12 * 10**6, transcendentals=2 * 10**6),
    )(page_map, hit_pages, suffix_lengths, q, suffix, kv_pool, out_weight)
    return out[None]


def solution(mesh):
    in_specs = (
        P(("groups", "pool"), None, "tp", None),
        P(("groups", "pool"), None, None, None),
        P(("groups", "pool", "tp"), None, None, None),
        P("groups"),
        P("groups", None),
        P(("groups", "pool")),
        P("tp", None),
    )
    out_specs = P(("groups", "pool"), "tp", None)
    return jax.shard_map(
        functools.partial(per_device, mesh.shape["pool"], mesh.shape["tp"]),
        mesh=mesh, in_specs=in_specs, out_specs=out_specs, check_vma=False,
    )
```

```python
import functools
import math

import jax
import jax.numpy as jnp
from jax import lax
from jax.experimental import pallas as pl
from jax.experimental.pallas import tpu as pltpu
from jax.sharding import PartitionSpec as P

CAP = 2
STAT = 8
LANES = 128
NEG_FILL = -1e30
MESH = pl.DeviceIdType.MESH
F32 = jnp.float32
BF16 = jnp.bfloat16


def kernel(
    pools, tps, block,
    map_ref, hit_ref, len_ref, q_ref, suf_ref, pool_ref, w_hbm,
    out_ref,
    w_ref, kv, kv_send, q_all, o_send, o_recv, s_send, s_recv, o_suf, attn, part, own, c_send, c_up, c_dn,
    w_sem, kv_ss, kv_rs, q_ss, q_rs, o_ss, o_rs, s_ss, s_rs, c_ss, up_rs, dn_rs,
):
    me_p, me = lax.axis_index("pool"), lax.axis_index("tp")
    pages_dev, kv_heads, page, width = pool_ref.shape
    hd = width // 2
    heads, rows, _ = q_ref.shape
    hits = hit_ref.shape[1]
    group = heads * tps // kv_heads
    blocks = own.shape[0]
    rows_dev = rows // tps
    scale = math.log2(math.e) / math.sqrt(hd)

    w_copy = pltpu.make_async_copy(w_hbm, w_ref, w_sem)
    w_copy.start()

    barrier = pltpu.get_barrier_semaphore()
    for d in range(1, pools):
        pl.semaphore_signal(barrier, inc=1, device_id={"pool": lax.rem(me_p + d, pools)}, device_id_type=MESH)
    for d in range(1, tps):
        pl.semaphore_signal(barrier, inc=1, device_id={"tp": lax.rem(me + d, tps)}, device_id_type=MESH)
    pl.semaphore_wait(barrier, pools + tps - 2)

    def q_copy(d):
        return pltpu.make_async_remote_copy(
            src_ref=q_ref, dst_ref=q_all.at[d - 1], send_sem=q_ss.at[d - 1], recv_sem=q_rs.at[d - 1],
            device_id={"tp": lax.rem(me + d, tps)}, device_id_type=MESH,
        )

    def kv_copy(d):
        return pltpu.make_async_remote_copy(
            src_ref=kv_send.at[d - 1], dst_ref=kv.at[d], send_sem=kv_ss.at[d - 1], recv_sem=kv_rs.at[d - 1],
            device_id={"pool": lax.rem(me_p + d, pools)}, device_id_type=MESH,
        )

    base = (me_p * tps + me) * pages_dev

    def choose(session):
        def body(i, carry):
            first, second, rank = carry
            local = map_ref[hit_ref[session, i]] - base
            owned = jnp.logical_and(local >= 0, local < pages_dev)
            first = jnp.where(jnp.logical_and(owned, rank == 0), local, first)
            second = jnp.where(jnp.logical_and(owned, rank == 1), local, second)
            return first, second, rank + owned.astype(jnp.int32)

        zero = jnp.int32(0)
        return lax.fori_loop(0, hits, body, (zero, zero, zero), unroll=hits <= 16)[:2]

    order = sorted(range(1, pools), key=lambda d: -min(d, pools - d))
    for d in order:
        first, second = choose(lax.rem(me_p + d, pools))
        kv_send[d - 1, 0] = pool_ref[first]
        kv_send[d - 1, 1] = pool_ref[second]
        kv_copy(d).start()
    for d in range(1, tps):
        q_copy(d).start()
    first, second = choose(me_p)
    kv[0, 0] = pool_ref[first]
    kv[0, 1] = pool_ref[second]

    bases = [(lax.rem(me_p + pools - d, pools) * tps + me) * pages_dev for d in range(pools)]

    def count(i, carry):
        physical = map_ref[hit_ref[me_p, i]]
        return tuple(
            c + jnp.logical_and(physical >= b, physical < b + pages_dev).astype(jnp.int32)
            for c, b in zip(carry, bases)
        )

    counts = lax.fori_loop(0, hits, count, tuple(jnp.int32(0) for _ in bases), unroll=hits <= 16)
    lane2 = lax.broadcasted_iota(jnp.int32, (1, CAP * page), 1)
    biases = [
        jnp.where(lane2 < page, jnp.where(c > 0, 0.0, NEG_FILL), jnp.where(c > 1, 0.0, NEG_FILL)).astype(F32)
        for c in counts
    ]

    def softmax(scores, values):
        top = functools.reduce(jnp.maximum, scores)
        peak = jnp.max(top, axis=1, keepdims=True) * scale
        weights = [jnp.exp2(s * scale - peak) for s in scores]
        total = jnp.sum(functools.reduce(jnp.add, weights), axis=1, keepdims=True)
        acc = functools.reduce(
            jnp.add,
            [jnp.dot(x.astype(BF16), v, preferred_element_type=F32) for x, v in zip(weights, values)],
        )
        return acc / total, peak + jnp.log2(total)

    def dot_t(a, b):
        return lax.dot_general(a, b, (((1,), (1,)), ((), ())), preferred_element_type=F32)

    q_own = q_ref[...].reshape(heads * rows, hd)
    scores = dot_t(q_own, suf_ref[:, :hd])
    row = lax.broadcasted_iota(jnp.int32, (heads * rows, rows), 0)
    column = lax.broadcasted_iota(jnp.int32, (heads * rows, rows), 1)
    scores = jnp.where(column * heads <= row, scores, NEG_FILL)
    att_suf, lse_suf = softmax([scores], [suf_ref[:, hd:]])
    o_suf[...] = att_suf

    def prefix(q, rank):
        g = lax.div(rank * heads, group)
        keys, values = [], []
        for d in range(pools):
            both = kv[d, :, g].reshape(CAP * page, width)
            keys.append(both[:, :hd])
            values.append(both[:, hd:])
        return softmax([dot_t(q, k) + b for k, b in zip(keys, biases)], values)

    for d in range(1, pools):
        kv_copy(d).wait_recv()
    for d in range(s_recv.shape[0]):
        if d >= tps - 1:
            s_recv[d] = jnp.zeros_like(s_recv[d])

    def o_copy(d):
        return pltpu.make_async_remote_copy(
            src_ref=o_send.at[d - 1], dst_ref=o_recv.at[d - 1], send_sem=o_ss.at[d - 1], recv_sem=o_rs.at[d - 1],
            device_id={"tp": lax.rem(me + d, tps)}, device_id_type=MESH,
        )

    def s_copy(d):
        return pltpu.make_async_remote_copy(
            src_ref=s_send.at[d - 1], dst_ref=s_recv.at[d - 1], send_sem=s_ss.at[d - 1], recv_sem=s_rs.at[d - 1],
            device_id={"tp": lax.rem(me + d, tps)}, device_id_type=MESH,
        )

    lane = lax.broadcasted_iota(jnp.int32, (rows, LANES), 1)

    @pl.loop(1, tps)
    def _(d):
        q_copy(tps - d).wait_recv()
        att, lse = prefix(q_all[tps - d - 1].reshape(heads * rows, hd), lax.rem(me + d, tps))
        o_send[d - 1] = att.astype(BF16).reshape(heads, rows, hd)
        o_copy(d).start()
        tile = jnp.zeros((rows, LANES), F32)
        for j in range(heads):
            tile = jnp.where(lane == j, lse[j * rows:(j + 1) * rows], tile)
        s_send[d - 1] = tile.T[:STAT]
        s_copy(d).start()

    att_own, lse_own = prefix(q_own, me)

    for d in range(1, tps):
        o_copy(d).wait_recv()
        s_copy(d).wait_recv()
    stats = s_recv[...].reshape(LANES, rows).T
    tokens = rows // heads
    place = lax.broadcasted_iota(jnp.int32, (rows, 1), 0)
    pick_to = lax.broadcasted_iota(jnp.int32, (tokens, rows), 0) * heads
    pick_from = lax.broadcasted_iota(jnp.int32, (tokens, rows), 1)
    for j in range(heads):
        here = slice(j * rows, (j + 1) * rows)
        logs = [lse_own[here], lse_suf[here]] + [
            stats[:, (d - 1) * STAT + j:(d - 1) * STAT + j + 1] for d in range(1, tps)
        ]
        parts = [att_own[here], o_suf[here]] + [o_recv[d - 1, j].astype(F32) for d in range(1, tps)]
        peak = functools.reduce(jnp.maximum, logs)
        shares = [jnp.exp2(x - peak) for x in logs]
        total = functools.reduce(jnp.add, shares)
        mixed = functools.reduce(jnp.add, [s * o for s, o in zip(shares, parts)]) / total
        live = place + j * rows < len_ref[0] * heads
        mixed = jnp.where(live, mixed, 0.0).astype(BF16)
        for h in range(heads):
            picks = jnp.where(pick_to + h == pick_from, 1.0, 0.0).astype(BF16)
            attn[j * tokens:(j + 1) * tokens, h * hd:(h + 1) * hd] = jnp.dot(
                picks, mixed, preferred_element_type=F32
            ).astype(BF16)

    w_copy.wait()

    def c_copy(t, b, up):
        landing, sem, to = (c_up, up_rs, me + 1) if up else (c_dn, dn_rs, me + tps - 1)
        return pltpu.make_async_remote_copy(
            src_ref=c_send.at[t, b], dst_ref=landing.at[t, b], send_sem=c_ss.at[t, b], recv_sem=sem.at[t, b],
            device_id={"tp": lax.rem(to, tps)}, device_id_type=MESH,
        )

    def pass_on(t, b, up):
        first_one = me == 0 if up else me == tps - 1

        @pl.when(first_one)
        def _():
            c_send[t, b] = part[t].astype(BF16)

        @pl.when(jnp.logical_not(first_one))
        def _():
            c_copy(t, b, up).wait_recv()
            landing = c_up if up else c_dn
            c_send[t, b] = (part[t] + landing[t, b].astype(F32)).astype(BF16)

        c_copy(t, b, up).start()

    @pl.loop(0, blocks)
    def _(b):
        columns = pl.ds(pl.multiple_of(b * block, block), block)
        product = jnp.dot(attn[...], w_ref[:, columns], preferred_element_type=F32)
        for t in range(tps):
            part[t] = product[t * rows_dev:(t + 1) * rows_dev]
        own[b] = part[me]
        for far in range(tps - 1, 0, -1):
            @pl.when(me + far < tps)
            def _():
                pass_on(me + far, b, True)

            @pl.when(me >= far)
            def _():
                pass_on(me - far, b, False)

    @pl.loop(0, blocks)
    def _(b):
        @pl.when(me > 0)
        def _():
            c_copy(me, b, True).wait_recv()
            own[b] = own[b] + c_up[me, b].astype(F32)

        @pl.when(me < tps - 1)
        def _():
            c_copy(me, b, False).wait_recv()
            own[b] = own[b] + c_dn[me, b].astype(F32)

        out_ref[:, pl.ds(pl.multiple_of(b * block, block), block)] = own[b].astype(BF16)

    for d in range(1, pools):
        kv_copy(d).wait_send()
    for d in range(1, tps):
        q_copy(d).wait_send()
        o_copy(d).wait_send()
        s_copy(d).wait_send()

    @pl.loop(0, blocks)
    def _(b):
        for far in range(1, tps):
            @pl.when(me + far < tps)
            def _():
                c_copy(me + far, b, True).wait_send()

            @pl.when(me >= far)
            def _():
                c_copy(me - far, b, False).wait_send()


def per_device(pools, tps, queries, suffix_kv, kv_pool, page_map, hit_pages, suffix_lengths, out_weight):
    pages_dev, kv_heads, page, width = kv_pool.shape
    hd = width // 2
    rows, heads = queries.shape[1], queries.shape[2]
    model = out_weight.shape[1]
    block = min(1024, model)
    blocks = model // block
    rows_dev = rows // tps
    group = heads * tps // kv_heads
    q = queries.reshape(heads, rows, hd)
    suffix = lax.dynamic_index_in_dim(
        suffix_kv[0], lax.axis_index("tp") * heads // group, 1, keepdims=False
    )
    vmem = pl.BlockSpec(memory_space=pltpu.VMEM)
    smem = pl.BlockSpec(memory_space=pltpu.SMEM)
    dma = pltpu.SemaphoreType.DMA
    chain = (tps, blocks, rows_dev, block)
    out = pl.pallas_call(
        functools.partial(kernel, pools, tps, block),
        out_shape=jax.ShapeDtypeStruct((rows_dev, model), BF16),
        in_specs=[smem, smem, smem, vmem, vmem, vmem, pl.BlockSpec(memory_space=pl.ANY)],
        out_specs=vmem,
        scratch_shapes=[
            pltpu.VMEM(out_weight.shape, BF16),
            pltpu.VMEM((pools, CAP, kv_heads, page, width), BF16),
            pltpu.VMEM((pools - 1, CAP, kv_heads, page, width), BF16),
            pltpu.VMEM((tps - 1, heads, rows, hd), BF16),
            pltpu.VMEM((tps - 1, heads, rows, hd), BF16),
            pltpu.VMEM((tps - 1, heads, rows, hd), BF16),
            pltpu.VMEM((tps - 1, STAT, rows), F32),
            pltpu.VMEM((LANES // STAT, STAT, rows), F32),
            pltpu.VMEM((heads * rows, hd), F32),
            pltpu.VMEM((rows, heads * hd), BF16),
            pltpu.VMEM((tps, rows_dev, block), F32),
            pltpu.VMEM((blocks, rows_dev, block), F32),
            pltpu.VMEM(chain, BF16),
            pltpu.VMEM(chain, BF16),
            pltpu.VMEM(chain, BF16),
            dma,
            dma((pools - 1,)), dma((pools - 1,)),
            dma((tps - 1,)), dma((tps - 1,)),
            dma((tps - 1,)), dma((tps - 1,)),
            dma((tps - 1,)), dma((tps - 1,)),
            dma((tps, blocks)), dma((tps, blocks)), dma((tps, blocks)),
        ],
        compiler_params=pltpu.CompilerParams(
            collective_id=0, has_side_effects=True, vmem_limit_bytes=56 * 1024 * 1024
        ),
        cost_estimate=pl.CostEstimate(flops=3 * 10**9, bytes_accessed=12 * 10**6, transcendentals=2 * 10**6),
    )(page_map, hit_pages, suffix_lengths, q, suffix, kv_pool, out_weight)
    return out[None]


def solution(mesh):
    in_specs = (
        P(("groups", "pool"), None, "tp", None),
        P(("groups", "pool"), None, None, None),
        P(("groups", "pool", "tp"), None, None, None),
        P("groups"),
        P("groups", None),
        P(("groups", "pool")),
        P("tp", None),
    )
    out_specs = P(("groups", "pool"), "tp", None)
    return jax.shard_map(
        functools.partial(per_device, mesh.shape["pool"], mesh.shape["tp"]),
        mesh=mesh, in_specs=in_specs, out_specs=out_specs, check_vma=False,
    )
```
